512 devices in a mesh: expert: 64 (over x, y, core), head: 8 (over z).
Axes of the slice: x: 4, y: 8, z: 8, core: 2. Of those that a mesh axis runs over, the one named last changes fastest.
Arguments:
- tokens: bfloat16 [2, 1536, 4096], P(None, 'expert', 'head'), may hold values from -6 to 6
- queries: bfloat16 [2, 1536, 64, 576], P(None, 'expert', 'head'), may hold values from -10 to 10
- latent_cache: bfloat16 [1536, 16, 576], P('expert'), may hold values from -4 to 4
- lengths: int32 [1536], P('expert'), may hold values from 2 to 14, as said below
- expert_ids: int32 [2, 1536, 8], P(None, 'expert'), may hold values from 0 to 63, all different within a row; in each aligned block of 24 rows (0 to 23, 24 to 47, ..., all dimensions but the last counted through in order) at most 4 rows name the same one
- route_score: float32 [2, 1536, 8], P(None, 'expert'), may hold values from 0.05 to 1
- survive: int32 [1, 1536], P(None, 'expert'), may hold values 0 or 1
- destination: int32 [1, 1536], P(None, 'expert'), may hold values from 0 to 63, as said below
- w_gate: bfloat16 [64, 4096, 1024], P('expert', None, 'head'), may hold values from -0.09375 to 0.09375
- w_up: bfloat16 [64, 4096, 1024], P('expert', None, 'head'), may hold values from -0.09375 to 0.09375
- w_down: bfloat16 [64, 1024, 4096], P('expert', 'head'), may hold values from -0.1875 to 0.1875
- w_latent: bfloat16 [4096, 576], P('head'), may hold values from -0.09375 to 0.09375
- kv_gain: float32 [512], replicated, may hold values from 0.1 to 1.9
Outputs:
- attn_out: bfloat16 [2, 1536, 64, 512], P(None, 'expert', 'head')
- layer_out: bfloat16 [2, 1536, 4096], P(None, 'expert', 'head')
The draws below stay inside these ranges and needn't reach their ends.
Inputs may be any that keep to these rules, and one draw needn't show every extreme that they name: `expert_ids`: in the rows of one group at one step no expert is named more than 4 times. `lengths`: counts the current token. `destination`: at each step the rows that share a slot index r in all groups go to distinct groups, so every slot receives exactly one row; at each step, no group sends more than 1 row to any one group.
All inputs are finite; a program needn't handle non-finite values. No bound on the sum of `survive` on one device may be relied on, other than what follows from the above.
Results may differ from the reference program's by a relative error of at most 0.014.
Values may be sent and summed in bfloat16 or wider, within the bound.
No kernel may reach another device: no remote copies, remote signals or barrier semaphores. Data moves between devices by JAX's collectives and lax.ppermute only.
A program may use at most 64 MiB of HBM per device.

```python
import math
import jax
import jax.numpy as jnp
import numpy as np
from jax import lax

D = 4096
FF = 1024
HEADS = 64
LAT = 576
KVR = 512
TOPK = 8
STEPS = 2
ROWS = 24
CACHE = 16
EXPERTS = 64
ROWS_ALL = 1536
CAP = 4
N_EXPERT = 64
N_HEAD = 8


def draw_queries(key, part):
    key = jax.random.fold_in(key, 11)
    values = jnp.clip(jax.random.normal(key, (STEPS, ROWS_ALL, HEADS, LAT), jnp.float32), -4.0, 4.0)
    return values.astype(jnp.bfloat16)


def draw_latent_cache(key, part):
    key = jax.random.fold_in(key, 12)
    values = jnp.clip(jax.random.normal(key, (ROWS_ALL, CACHE, LAT), jnp.float32), -4.0, 4.0)
    return values.astype(jnp.bfloat16)


def draw_lengths(key, part):
    key = jax.random.fold_in(key, 13)
    key_first, key_second = jax.random.split(key)
    values = jax.random.randint(key_first, (ROWS_ALL,), 2, CACHE - STEPS + 1)
    top_index = jax.random.randint(key_second, (), 0, ROWS_ALL)
    return jnp.where(jnp.arange(ROWS_ALL) == top_index, CACHE - STEPS, values).astype(jnp.int32)


def destination_step(step_key):
    groups = ROWS_ALL // ROWS
    subkeys = jax.random.split(step_key, 3)
    first_perm = jax.random.permutation(subkeys[0], groups)
    second_perm = jax.random.permutation(subkeys[1], groups)
    rounds = (ROWS + groups - 1) // groups
    offsets = jnp.concatenate([jax.random.permutation(jax.random.fold_in(subkeys[2], index), groups) for index in range(rounds)])[:ROWS]
    target_table = (first_perm[:, None] + offsets[None, :]) % groups
    return second_perm[target_table].reshape(-1)


def draw_destination(key, part):
    key = jax.random.fold_in(key, 14)
    return jnp.stack([destination_step(jax.random.fold_in(key, index)) for index in range(STEPS - 1)]).astype(jnp.int32)


def touch_ends(drawn, stream_key, smallest, largest):
    longest = drawn.shape.index(max(drawn.shape))
    spots = []
    for shift in (0, 1):
        where = [jax.random.randint(jax.random.fold_in(stream_key, axis), (), 0, length) for axis, length in enumerate(drawn.shape)]
        where[longest] = (where[longest] + shift) % drawn.shape[longest]
        spots.append(tuple(where))
    return drawn.at[spots[0]].set(smallest).at[spots[1]].set(largest)


def steps_of(rng, shape, cuts, smallest, top_value):
    loudness = 1.0
    for dim, shards_of in cuts:
        draws = jax.random.uniform(jax.random.fold_in(jax.random.fold_in(rng, 6), dim), (shards_of,), jnp.float32, smallest / len(cuts), top_value / len(cuts))
        loudness = loudness * jnp.repeat(jnp.exp(draws), shape[dim] // shards_of).reshape((-1,) + (1,) * (len(shape) - 1 - dim))
    return loudness


def deal_out(stream_key, own, number, rows, count, top, limit, lean):
    order = jax.random.permutation(stream_key, count)
    packed, ordinary = portions_of(count, rows * top, limit, lean, True), portions_of(count, rows * top, limit, lean, False)
    places = jnp.arange(count)

    def named(sizes, rotation):
        used = int((sizes > 0).sum())
        fixed = max(1, used // 4)
        shifted = fixed + (places - fixed + rotation * (used - fixed)) % max(1, count - fixed)
        return jnp.zeros((count,), jnp.int32).at[order[jnp.where(places < fixed, places, shifted)]].set(jnp.asarray(sizes, jnp.int32))

    sizes = jnp.where(number % 4 == 0, named(packed, number // 4), named(ordinary, number - number // 4 - 1))
    mixed = jax.random.permutation(jax.random.fold_in(own, 3), count)
    source_of, taker = mixed[0:count // 2 * 2:2], mixed[1:count // 2 * 2:2]
    room = jnp.minimum(sizes[source_of] - 1, limit - sizes[taker]) // 2
    room = jnp.where((source_of == order[0]) | (taker == order[0]) | (sizes[taker] == 0), 0, jnp.maximum(room, 0))
    shifted = jax.random.randint(jax.random.fold_in(own, 4), (count // 2,), 0, 1 << 20) % (room + 1)
    sizes = sizes.at[source_of].add(-shifted).at[taker].add(shifted)
    items = jnp.searchsorted(jnp.cumsum(sizes), jnp.arange(rows * top), side="right").astype(jnp.int32)
    table = items.reshape(top, rows).T
    table = table[jax.random.permutation(jax.random.fold_in(own, 1), rows)]
    rotation = jax.random.randint(jax.random.fold_in(own, 2), (rows, 1), 0, top)
    return jnp.take_along_axis(table, (jnp.arange(top)[None, :] + rotation) % top, axis=1)


def portions_of(count, total, reach, lean, full):
    weights = [(1 << 20) // math.isqrt(standing ** lean) + 1 for standing in range(1, count + 1)]
    largest = reach if full else min(reach, max(-(-total // count), total * weights[0] // sum(weights)))
    least = 1 if total - largest >= count - 1 else 0
    holding, surplus = [largest] + [least] * (count - 1), total - largest - least * (count - 1)
    while surplus > 0:
        candidates = [i for i in range(1, count) if holding[i] < largest] or [i for i in range(1, count) if holding[i] < reach]
        mass, left = sum([weights[i] for i in candidates]), surplus
        for i in candidates:
            more = min(reach - holding[i], max(1, left * weights[i] // mass), surplus)
            holding[i] = holding[i] + more
            surplus = surplus - more
    return np.array(holding)


def scatter_about(key, extent, width, reach, cuts=(), dtype=jnp.bfloat16):
    level = steps_of(key, extent, cuts, -0.22, 0.18) if cuts else 1.0
    entries = jax.random.normal(key, extent, jnp.float32) * width * level
    return jnp.minimum(jnp.maximum(entries, -reach), reach).astype(dtype)


def setup_inputs(seed: int = 0) -> dict:
    keys = jax.random.split(jax.random.key(seed), 14)
    tokens = scatter_about(keys[0], (STEPS, ROWS_ALL, D), 1.0, 6.0, ((1, 64), (2, 8)))
    queries = draw_queries(jax.random.fold_in(keys[13], 71), 0)
    latent_cache = draw_latent_cache(jax.random.fold_in(keys[13], 71), 0)
    lengths = draw_lengths(jax.random.fold_in(keys[13], 71), 0)
    expert_ids_keys = jax.random.split(jax.random.fold_in(keys[4], 1), STEPS * ROWS_ALL // ROWS)
    expert_ids_turns = jax.random.permutation(jax.random.fold_in(keys[4], 3), STEPS * ROWS_ALL // ROWS)
    expert_ids = jax.vmap(lambda own, number: deal_out(jax.random.fold_in(keys[4], 2), own, number, ROWS, EXPERTS, TOPK, CAP, 2))(expert_ids_keys, expert_ids_turns).reshape((STEPS, ROWS_ALL, TOPK))
    route_score = jnp.clip(0.05 + 0.95 * jax.random.uniform(keys[5], (STEPS, ROWS_ALL, TOPK), jnp.float32) ** steps_of(keys[5], (STEPS, ROWS_ALL, TOPK), ((1, 64),), -0.2, 0.2), 0.05, 1.0)
    survive = touch_ends((jax.random.randint(keys[6], (STEPS - 1, ROWS_ALL), 0, 4) < 3).astype(jnp.int32), jax.random.fold_in(keys[6], 1), 0, 1)
    destination = draw_destination(jax.random.fold_in(keys[13], 71), 0)
    w_gate = scatter_about(keys[8], (EXPERTS, D, FF), D ** -0.5, 0.09375, ((0, 64), (2, 8)))
    w_up = scatter_about(keys[9], (EXPERTS, D, FF), D ** -0.5, 0.09375, ((0, 64), (2, 8)))
    w_down = scatter_about(keys[10], (EXPERTS, FF, D), FF ** -0.5, 0.1875, ((0, 64), (1, 8)))
    w_latent = scatter_about(keys[11], (D, LAT), D ** -0.5, 0.09375, ((0, 8),))
    kv_gain = jnp.clip(1.0 + 0.18 * jax.random.normal(keys[12], (KVR,), jnp.float32), 0.1, 1.9)
    return dict(tokens=tokens, queries=queries, latent_cache=latent_cache, lengths=lengths, expert_ids=expert_ids, route_score=route_score, survive=survive, destination=destination, w_gate=w_gate, w_up=w_up, w_down=w_down, w_latent=w_latent, kv_gain=kv_gain)


SCORE_SCALE = 192.0 ** (-0.5)
ROUTE_SCALE = 2.5
NORM_EPS = 1e-06

def attend(query, cache_now, lengths_now):
    scores = jnp.einsum('rhc,rpc->rhp', query.astype(jnp.float32), cache_now.astype(jnp.float32), precision=lax.Precision.HIGHEST) * SCORE_SCALE
    in_range = jnp.arange(CACHE)[None, None, :] < lengths_now[:, None, None]
    row_top = lax.optimization_barrier(jnp.max(jnp.where(in_range, scores, -1e+30), axis=2, keepdims=True))
    exp_terms = jnp.where(in_range, jnp.exp(scores - row_top), 0.0)
    denominator = lax.optimization_barrier(jnp.sum(exp_terms, axis=2, keepdims=True))
    denominator = jnp.where(lengths_now[:, None, None] > 0, denominator, 1.0)
    weights = (exp_terms / denominator).astype(jnp.bfloat16)
    values = cache_now[:, :, :KVR]
    return jnp.einsum('rhp,rpc->rhc', weights.astype(jnp.float32), values.astype(jnp.float32), precision=lax.Precision.HIGHEST).astype(jnp.bfloat16)

def expert_apply(inputs):
    rows_in, gate_w, up_w, down_w = inputs
    gate_acts = jnp.dot(rows_in, gate_w, preferred_element_type=jnp.float32)
    up_acts = jnp.dot(rows_in, up_w, preferred_element_type=jnp.float32)
    hidden = (jax.nn.silu(gate_acts) * up_acts).astype(jnp.bfloat16)
    blocks = hidden.reshape(hidden.shape[0], N_HEAD, FF // N_HEAD).astype(jnp.float32)
    down_blocks = down_w.reshape(N_HEAD, FF // N_HEAD, D).astype(jnp.float32)
    part_sums = jnp.einsum('snf,nfd->snd', blocks, down_blocks, precision=lax.Precision.HIGHEST).astype(jnp.bfloat16)
    part_sums = lax.optimization_barrier(part_sums)
    return lax.optimization_barrier(jnp.sum(part_sums.astype(jnp.float32), axis=1)).astype(jnp.bfloat16)

def reference(tokens, queries, latent_cache, lengths, expert_ids, route_score, survive, destination, w_gate, w_up, w_down, w_latent, kv_gain):
    slot_in_group = (jnp.arange(ROWS_ALL) % ROWS).astype(jnp.int32)
    group_of = (jnp.arange(ROWS_ALL) // ROWS).astype(jnp.int32)
    cache_now = latent_cache
    lengths_now = lengths
    attended = []
    layered = []
    for section_index in range(STEPS):
        attended.append(attend(queries[section_index], cache_now, lengths_now))
        chosen = expert_ids[section_index]
        grouped = chosen.reshape(N_EXPERT, ROWS * TOPK)
        onehot = (grouped[:, :, None] == jnp.arange(EXPERTS)[None, None, :]).astype(jnp.int32)
        before = jnp.cumsum(onehot, axis=1) - onehot
        position = lax.optimization_barrier(jnp.sum(before * onehot, axis=2)).reshape(ROWS_ALL, TOPK)
        target = ((chosen * N_EXPERT + group_of[:, None]) * CAP + position).astype(jnp.int32).reshape(-1)
        source_rows = jnp.broadcast_to(tokens[section_index][:, None, :], (ROWS_ALL, TOPK, D)).reshape(-1, D)
        buffers = jnp.zeros((EXPERTS * N_EXPERT * CAP, D), jnp.bfloat16).at[target].set(source_rows)
        results = lax.map(expert_apply, (buffers.reshape(EXPERTS, N_EXPERT * CAP, D), w_gate, w_up, w_down))
        picked = results.reshape(-1, D)[target].reshape(ROWS_ALL, TOPK, D)
        share_raw = route_score[section_index]
        route_weight = ROUTE_SCALE * share_raw / lax.optimization_barrier(jnp.sum(share_raw, axis=1, keepdims=True))
        mixed_out = tokens[section_index].astype(jnp.float32) + jnp.einsum('rk,rkd->rd', route_weight, picked.astype(jnp.float32), precision=lax.Precision.HIGHEST)
        layer_row = mixed_out.astype(jnp.bfloat16)
        layered.append(layer_row)
        if section_index + 1 < STEPS:
            whole_sum = jnp.dot(layer_row, w_latent, preferred_element_type=jnp.float32)
            leading = whole_sum[:, :KVR]
            norm_scale = lax.rsqrt(lax.optimization_barrier(jnp.mean(leading * leading, axis=1, keepdims=True)) + NORM_EPS)
            latent = jnp.concatenate([leading * norm_scale * kv_gain, whole_sum[:, KVR:]], axis=1).astype(jnp.bfloat16)
            at_length = jnp.arange(CACHE)[None, :, None] == lengths_now[:, None, None]
            cache_now = jnp.where(at_length, latent[:, None, :], cache_now)
            lengths_now = lengths_now + 1
            moved = (destination[section_index] * ROWS + slot_in_group).astype(jnp.int32)
            cache_now = jnp.zeros_like(cache_now).at[moved].set(cache_now)
            kept = jnp.where(survive[section_index] == 1, lengths_now, 0).astype(jnp.int32)
            lengths_now = jnp.zeros_like(lengths_now).at[moved].set(kept)
    return (jnp.stack(attended), jnp.stack(layered))
```

```python
import jax
import jax.numpy as jnp
from jax import lax
from jax.sharding import PartitionSpec as P

KVR = 512
TOPK = 8
STEPS = 2
CAP = 4

SCORE_SCALE = 192.0 ** (-0.5)
ROUTE_SCALE = 2.5
NORM_EPS = 1e-06
LOW = -1e30

BF = jnp.bfloat16
F32 = jnp.float32


def dot(a, b, dims, precision=None):
    return lax.dot_general(a, b, (dims, ((), ())), precision=precision, preferred_element_type=F32)


def exchange(x, axis):
    return lax.all_to_all(x, axis, split_axis=0, concat_axis=0, tiled=True)


def together(*arrays):
    return lax.optimization_barrier(arrays)


def routing(ids, score, groups):
    rows = ids.shape[0]
    column = lax.broadcasted_iota(jnp.int32, (1, 1, groups * CAP), 2)
    hit = ids[:, :, None] == column // CAP
    named = jnp.any(hit, axis=1)
    share = ROUTE_SCALE * score / jnp.sum(score, axis=1, keepdims=True)
    weight = jnp.sum(jnp.where(hit, share[:, :, None], 0.0), axis=1)
    earlier = (
        lax.broadcasted_iota(jnp.int32, (rows, rows), 1)
        < lax.broadcasted_iota(jnp.int32, (rows, rows), 0)
    ).astype(BF)
    before = dot(earlier, named.astype(BF), ((1,), (0,)))
    place = named & (before == (column[0] % CAP).astype(F32))
    return place.astype(BF), jnp.where(place, weight, 0.0)


def softmax_values(parts):
    top = parts[0][0].max(axis=1, keepdims=True)
    for scores, _, _ in parts[1:]:
        top = jnp.maximum(top, scores.max(axis=1, keepdims=True))
    terms = [jnp.where(mask, jnp.exp(scores - top), 0.0) for scores, mask, _ in parts]
    total = sum(t.sum(axis=1, keepdims=True) for t in terms)
    total = jnp.where(total > 0, total, 1.0)
    return sum(
        dot((t / total).astype(BF), values, ((1,), (0,)))
        for t, (_, _, values) in zip(terms, parts)
    )


def on_device(
    tokens,
    queries,
    latent_cache,
    lengths,
    expert_ids,
    route_score,
    survive,
    destination,
    w_gate,
    w_up,
    w_down,
    w_latent,
    kv_gain,
):
    groups = lax.axis_size("expert")
    heads_axis = lax.axis_size("head")
    rows, positions, width = latent_cache.shape
    heads = queries.shape[2]
    feats = tokens.shape[2]
    block = w_gate.shape[2]
    wide = 768

    route = [routing(expert_ids[s], route_score[s], groups) for s in range(STEPS)]

    def send(s):
        return dot(route[s][0], tokens[s], ((0,), (0,))).astype(BF)

    arrived0 = exchange(send(0).reshape(groups, CAP, feats), "expert")
    rows0 = lax.all_gather(arrived0.reshape(groups * CAP, feats), "head", axis=1, tiled=True)

    down_slices = w_down[0].reshape(block, heads_axis, feats).transpose(1, 0, 2)
    down_slices, arrived0 = together(down_slices, arrived0)
    down = exchange(down_slices, "head").reshape(heads_axis * block, feats)

    alive = survive[0] == 1
    eye = jnp.eye(rows, wide - width, dtype=BF)
    target = (destination[0][:, None] == jnp.arange(groups)[None, :]).astype(BF)
    share = positions // heads_axis
    first = lax.axis_index("head") * share
    held = lax.dynamic_slice_in_dim(latent_cache, first, share, axis=1)
    spot = first + lax.broadcasted_iota(jnp.int32, (rows, share), 1)
    valid = ((spot < lengths[:, None]) & alive[:, None]).astype(BF)
    marked = jnp.concatenate([held, valid[:, :, None] * eye[:, None, :]], axis=2)
    packed = dot(target, marked.reshape(rows, share * wide), ((0,), (0,))).astype(BF)
    piece = share * wide // CAP
    both = jnp.concatenate(
        [send(1).reshape(groups, CAP, feats), packed.reshape(groups, CAP, piece)], axis=2
    )
    both, down = together(both, down)
    both = exchange(both, "expert")
    rows1 = lax.all_gather(
        both[:, :, :feats].reshape(groups * CAP, feats), "head", axis=1, tiled=True
    )
    pieces = both[:, :, feats:].reshape(groups * CAP, piece)
    pieces, rows1 = together(pieces, rows1)
    moved = lax.all_gather(pieces, "head", axis=0, tiled=True)
    moved = moved.reshape(heads_axis * groups * share, wide)

    q0 = queries[0].reshape(rows * heads, width)
    keys0 = latent_cache.reshape(rows * positions, width)
    row_of = lax.broadcasted_iota(jnp.int32, (rows, 1, rows, positions), 0)
    key_of = lax.broadcasted_iota(jnp.int32, (rows, 1, rows, positions), 2)
    spot = lax.broadcasted_iota(jnp.int32, (rows, 1, rows, positions), 3)
    mask0 = (row_of == key_of) & (spot < lengths[:, None, None, None])
    mask0 = jnp.broadcast_to(mask0, (rows, heads, rows, positions)).reshape(
        rows * heads, rows * positions
    )
    scores0 = jnp.where(mask0, dot(q0, keys0, ((1,), (1,))) * SCORE_SCALE, LOW)
    attn0 = softmax_values([(scores0, mask0, keys0[:, :KVR])]).astype(BF)

    def hidden_of(x):
        gate = jnp.dot(x, w_gate[0], preferred_element_type=F32)
        up = jnp.dot(x, w_up[0], preferred_element_type=F32)
        return (jax.nn.silu(gate) * up).astype(BF)

    def everywhere(x):
        return exchange(jnp.broadcast_to(x[None], (heads_axis,) + x.shape), "head")

    def down_of(parts):
        whole = parts.transpose(1, 0, 2).reshape(groups * CAP, heads_axis * block)
        return jnp.dot(whole, down, preferred_element_type=F32).astype(BF).reshape(groups, CAP, feats)

    def combine(s, back):
        back = back.reshape(groups * CAP, feats).astype(F32)
        mixed = dot(route[s][1], back, ((1,), (0,)), precision=lax.Precision.HIGHEST)
        return (tokens[s].astype(F32) + mixed).astype(BF)

    layer0 = combine(0, exchange(down_of(everywhere(hidden_of(rows0))), "expert"))

    part = jnp.dot(layer0, w_latent, preferred_element_type=F32).astype(BF)
    lanes = 128
    chunks = -(-width // lanes)
    part = jnp.pad(part, ((0, 0), (0, chunks * lanes - width)))
    part = [part[:, c * lanes : (c + 1) * lanes] for c in range(chunks)]
    shared = everywhere(jnp.concatenate([hidden_of(rows1)] + part, axis=0))
    sums = shared[:, groups * CAP :].astype(F32).sum(axis=0)
    whole_sum = jnp.concatenate([sums[c * rows : (c + 1) * rows] for c in range(chunks)], axis=1)
    leading = whole_sum[:, :KVR]
    norm = lax.rsqrt(jnp.mean(leading * leading, axis=1, keepdims=True) + NORM_EPS)
    latent = jnp.concatenate(
        [
            (leading * norm * kv_gain).astype(BF),
            whole_sum[:, KVR:width].astype(BF),
            alive.astype(BF)[:, None] * eye,
        ],
        axis=1,
    )
    sent = dot(target, jnp.pad(latent, ((0, 0), (0, 1024 - wide))), ((0,), (0,))).astype(BF)
    answers1 = down_of(shared[:, : groups * CAP])
    last = exchange(
        jnp.concatenate([answers1, sent.reshape(groups, CAP, 1024 // CAP)], axis=2), "expert"
    )
    layer1 = combine(1, last[:, :, :feats])
    fresh = last[:, :, feats:].reshape(groups, 1024)[:, :wide]

    q1 = queries[1].reshape(rows * heads, width)
    eye = jnp.repeat(eye, heads, axis=0)
    parts = []
    for keys in (moved, fresh):
        mask = dot(eye, keys[:, width:], ((1,), (1,))) > 0.5
        scores = dot(q1, keys[:, :width], ((1,), (1,))) * SCORE_SCALE
        parts.append((jnp.where(mask, scores, LOW), mask, keys[:, :KVR]))
    attn1 = softmax_values(parts).astype(BF)

    attn = jnp.stack([attn0, attn1]).reshape(STEPS, rows, heads, KVR)
    return attn, jnp.stack([layer0, layer1])


def solution(mesh):
    return jax.shard_map(
        on_device,
        mesh=mesh,
        in_specs=(
            P(None, "expert", "head"),
            P(None, "expert", "head", None),
            P("expert", None, None),
            P("expert"),
            P(None, "expert", None),
            P(None, "expert", None),
            P(None, "expert"),
            P(None, "expert"),
            P("expert", None, "head"),
            P("expert", None, "head"),
            P("expert", "head", None),
            P("head", None),
            P(),
        ),
        out_specs=(P(None, "expert", "head", None), P(None, "expert", "head")),
        check_vma=False,
    )
```

```python
import jax
import jax.numpy as jnp
from jax import lax
from jax.experimental import pallas as pl
from jax.experimental.pallas import tpu as pltpu
from jax.sharding import PartitionSpec as P

KVR = 512
TOPK = 8
STEPS = 2
CAP = 4
ROWS = 24
LAT = 576
CACHE = 16
LANES = 128

SCORE_SCALE = 192.0 ** (-0.5)
ROUTE_SCALE = 2.5
NORM_EPS = 1e-06
LOW = -1e30

BF = jnp.bfloat16
F32 = jnp.float32


def dot(a, b, dims, precision=None):
    return lax.dot_general(a, b, (dims, ((), ())), precision=precision, preferred_element_type=F32)


def exchange(x, axis):
    return lax.all_to_all(x, axis, split_axis=0, concat_axis=0, tiled=True)


def together(*arrays):
    return lax.optimization_barrier(arrays)


def places_of(ids, groups, per):
    rows = ids.shape[0]
    column = lax.broadcasted_iota(jnp.int32, (1, 1, groups * per), 2)
    hit = ids[:, :, None] == column // per
    named = jnp.any(hit, axis=1)
    earlier = (
        lax.broadcasted_iota(jnp.int32, (rows, rows), 1)
        < lax.broadcasted_iota(jnp.int32, (rows, rows), 0)
    ).astype(BF)
    before = dot(earlier, named.astype(BF), ((1,), (0,)))
    return named & (before == (column[0] % CAP).astype(F32)), hit


def mix_of(ids, score, groups):
    place, hit = places_of(ids, groups, CAP)
    share = ROUTE_SCALE * score / jnp.sum(score, axis=1, keepdims=True)
    weight = jnp.sum(jnp.where(hit, share[:, :, None], 0.0), axis=1)
    return jnp.where(place, weight, 0.0)


def softmax_values(parts):
    top = parts[0][0].max(axis=1, keepdims=True)
    for scores, _, _ in parts[1:]:
        top = jnp.maximum(top, scores.max(axis=1, keepdims=True))
    terms = [jnp.where(mask, jnp.exp(scores - top), 0.0) for scores, mask, _ in parts]
    total = sum(t.sum(axis=1, keepdims=True) for t in terms)
    total = jnp.where(total > 0, total, 1.0)
    return sum(
        dot((t / total).astype(BF), values, ((1,), (0,)))
        for t, (_, _, values) in zip(terms, parts)
    )


def expert_kernel(x, gate_w, up_w, down_w, out, x_in, wide_w, narrow_w, made, *sems):
    feats, block = gate_w.shape[1:]
    count = out.shape[0]
    rows, span = x_in.shape
    step = feats // 4
    starts = range(0, feats, step)

    def fetch(k, source, target):
        copy = pltpu.make_async_copy(source, target, sems[k])
        copy.start()
        return copy

    lots, gates, ups = [], [], []
    for c, at in enumerate(starts):
        part = pl.ds(at, step)
        if at < span:
            lots.append(fetch(c, x.at[:, part], x_in.at[:, part]))
        gates.append(fetch(4 + c, gate_w.at[0, part], wide_w.at[part, pl.ds(0, block)]))
        ups.append(fetch(8 + c, up_w.at[0, part], wide_w.at[part, pl.ds(block, block)]))
    narrow = fetch(12, down_w.at[0], narrow_w)
    sums = [0.0] * (feats // span)
    for c, at in enumerate(starts):
        if at < span:
            lots[c].wait()
        gates[c].wait()
        ups[c].wait()
        lanes = at % span
        sums[at // span] += jnp.dot(
            x_in[:, lanes : lanes + step], wide_w[at : at + step], preferred_element_type=F32
        )
    total = sums[0]
    if len(sums) == 2:
        total = total + jnp.concatenate([sums[1][CAP:], sums[1][:CAP]], axis=0)
    hidden = (jax.nn.silu(total[:, :block]) * total[:, block:]).astype(BF)
    if len(sums) == 2:
        line = lax.broadcasted_iota(jnp.int32, (count, rows), 0)
        column = lax.broadcasted_iota(jnp.int32, (count, rows), 1)
        keep = (line + line // CAP * CAP == column).astype(BF)
        hidden = jnp.dot(keep, hidden, preferred_element_type=F32).astype(BF)
    narrow.wait()
    sent = []
    for c, at in enumerate(starts):
        made[:, at : at + step] = jnp.dot(
            hidden, narrow_w[:, at : at + step], preferred_element_type=F32
        ).astype(BF)
        part = pl.ds(at, step)
        sent.append(fetch(13 + c, made.at[:, part], out.at[:, part]))
    for copy in sent:
        copy.wait()


def expert_part(x, span, count, w_gate, w_up, w_down, *waits):
    feats, block = w_gate.shape[1:]

    def kernel(*refs):
        refs = refs[:4] + refs[4 + len(waits) :]
        expert_kernel(*refs)

    return pl.pallas_call(
        kernel,
        out_shape=jax.ShapeDtypeStruct((count, feats), BF),
        in_specs=[pl.BlockSpec(memory_space=pltpu.HBM)] * (4 + len(waits)),
        out_specs=pl.BlockSpec(memory_space=pltpu.HBM),
        scratch_shapes=[
            pltpu.VMEM((x.shape[0], span), BF),
            pltpu.VMEM((feats, 2 * block), BF),
            pltpu.VMEM((block, feats), BF),
            pltpu.VMEM((count, feats), BF),
        ]
        + [pltpu.SemaphoreType.DMA] * 17,
        compiler_params=pltpu.CompilerParams(vmem_limit_bytes=60 * 2**20),
        cost_estimate=pl.CostEstimate(
            flops=6 * count * feats * block,
            bytes_accessed=4 * count * feats + 6 * feats * block,
            transcendentals=count * block,
        ),
    )(x, w_gate, w_up, w_down, *waits)


def pack_kernel(places, tokens, targets, tiles, out):
    feats = tokens.shape[2]
    half = tokens.shape[0] // 2
    for c in range(half):
        lines = sum(
            jnp.dot(places[h], tokens[h * half + c], preferred_element_type=F32) for h in range(2)
        )
        out[:, c * feats : (c + 1) * feats] = lines.astype(BF)
    out[:, half * feats :] = jnp.dot(
        targets[...], tiles[...], preferred_element_type=F32
    ).astype(BF)


def collect_kernel(x, out):
    lines = x.shape[0]
    own = (
        lax.broadcasted_iota(jnp.int32, (ROWS, LANES), 1)
        == lax.broadcasted_iota(jnp.int32, (ROWS, LANES), 0) + (LAT - KVR)
    ).astype(BF)
    marked = (dot(own, x[:, LANES:], ((1,), (1,))) > 0.5).astype(BF)
    block = (
        lax.broadcasted_iota(jnp.int32, (lines, lines), 0) // 8
        == lax.broadcasted_iota(jnp.int32, (lines, lines), 1) // 8
    ).astype(BF)
    chosen = dot(marked, block, ((1,), (0,)))
    place = lax.broadcasted_iota(jnp.int32, (ROWS, lines), 1) % 8
    picks = [jnp.where((place == q) & (chosen > 0.5), 1.0, 0.0).astype(BF) for q in range(8)]
    found = [dot(pick, x[:, :LANES], ((1,), (0,))) for pick in picks]
    found += [dot(pick, x[:, LANES:], ((1,), (0,))) for pick in picks[: CACHE // 8]]
    out[...] = jnp.concatenate(found, axis=0).astype(BF)


def attend_kernel(earlier, query, fresh, *refs):
    caches, out = refs[:-1], refs[-1]
    out[0] = earlier[...]
    rows, wide = query.shape
    lanes = wide - KVR
    slot = lax.broadcasted_iota(jnp.int32, (rows, lanes), 0) // (rows // ROWS)
    lane = lax.broadcasted_iota(jnp.int32, (rows, lanes), 1)
    own = (lane == slot + (LAT - KVR)).astype(BF)
    tiles = KVR // lanes
    held = [x[...] for x in caches] if len(caches) > 1 else [caches[0][h] for h in range(8)]
    share = held[0].shape[0] // ROWS // (tiles + 1)
    values, rests = [], []
    for x in held:
        x = [x[at : at + ROWS] for at in range(0, x.shape[0], ROWS)]
        for p in range(share):
            values.append(jnp.concatenate(x[p * tiles : (p + 1) * tiles], axis=1))
            rests.append(x[share * tiles + p])
    old = jnp.concatenate(
        [jnp.concatenate(values, axis=0), jnp.concatenate(rests, axis=0)], axis=1
    )
    parts = []
    for keys in (old, fresh[...]):
        scores = dot(query[...], keys, ((1,), (1,))) * SCORE_SCALE
        mask = dot(own, keys[:, KVR:], ((1,), (1,))) > 0.5
        parts.append((jnp.where(mask, scores, LOW), mask, keys[:, :KVR]))
    out[1] = softmax_values(parts).astype(BF)


def on_device(
    tokens,
    queries,
    latent_cache,
    lengths,
    expert_ids,
    route_score,
    survive,
    destination,
    w_gate,
    w_up,
    w_down,
    w_latent,
    kv_gain,
):
    groups = lax.axis_size("expert")
    heads_axis = lax.axis_size("head")
    rows, positions, width = latent_cache.shape
    heads = queries.shape[2]
    feats = tokens.shape[2]
    wide = 640

    place, _ = places_of(expert_ids[0], groups, CAP)
    sending = dot(place.astype(BF), tokens[0], ((0,), (0,))).astype(BF)
    arrived0 = exchange(sending.reshape(groups, CAP, feats), "expert")
    rows0 = lax.all_gather(arrived0.reshape(groups * CAP, feats), "head", axis=1, tiled=True)

    def everywhere(x):
        return exchange(jnp.broadcast_to(x[None], (heads_axis,) + x.shape), "head")

    alive = survive[0] == 1
    eye = jnp.eye(rows, LANES - (width - KVR), dtype=BF)
    target = (destination[0][:, None] == jnp.arange(groups)[None, :]).astype(BF)
    share = positions // heads_axis
    tiles = KVR // LANES
    per = share * tiles
    first = lax.axis_index("head") * share
    held = lax.dynamic_slice_in_dim(latent_cache, first, share, axis=1)
    spot = first + lax.broadcasted_iota(jnp.int32, (rows, share), 1)
    valid = ((spot < lengths[:, None]) & alive[:, None]).astype(BF)
    rest = jnp.concatenate([held[:, :, KVR:], valid[:, :, None] * eye[:, None, :]], axis=2)
    rest = jnp.pad(rest, ((0, 0), (0, per - share), (0, 0)))
    cache_tiles = jnp.concatenate([held[:, :, :KVR].reshape(rows, per, LANES), rest], axis=2)
    cache_tiles = cache_tiles.transpose(1, 0, 2).reshape(per * rows, 2 * LANES)

    column = lax.broadcasted_iota(jnp.int32, (1, groups * per), 1)
    place8, _ = places_of(expert_ids[1], groups, per)
    places = jnp.stack(
        [jnp.where(column % per // CAP == h, place8, False).astype(BF).T for h in range(2)]
    )
    to = destination[0][:, None] == column // per
    targets = jnp.stack([to & (column % per == q) for q in range(per)])
    targets = targets.reshape(per * rows, groups * per).astype(BF).T

    own, arrived0, places, targets, cache_tiles = together(
        tokens[1], arrived0, places, targets, cache_tiles
    )
    both = pl.pallas_call(
        pack_kernel,
        out_shape=jax.ShapeDtypeStruct(
            (groups * per, heads_axis * feats // 2 + 2 * LANES), BF
        ),
        in_specs=[pl.BlockSpec(memory_space=pltpu.VMEM)] * 4,
        out_specs=pl.BlockSpec(memory_space=pltpu.VMEM),
        compiler_params=pltpu.CompilerParams(vmem_limit_bytes=32 * 2**20),
    )(places, everywhere(own), targets, cache_tiles)
    both = exchange(both.reshape(groups, per, both.shape[1]), "expert")
    both = both.reshape(groups * per, both.shape[2])

    parts0 = expert_part(rows0, heads_axis * feats, groups * CAP, w_gate, w_up, w_down)
    parts1 = expert_part(
        both, heads_axis * feats // 2, groups * CAP, w_gate, w_up, w_down, parts0
    )

    pieces = both[:, heads_axis * feats // 2 :]
    pieces, parts1 = together(pieces, parts1)
    pieces = pl.pallas_call(
        collect_kernel,
        out_shape=jax.ShapeDtypeStruct(((per + share) * rows, LANES), BF),
        in_specs=[pl.BlockSpec(memory_space=pltpu.VMEM)],
        out_specs=pl.BlockSpec(memory_space=pltpu.VMEM),
    )(pieces)
    right = [(i, (i + 1) % heads_axis) for i in range(heads_axis)]
    left = [(i, (i - 1) % heads_axis) for i in range(heads_axis)]
    ahead, behind = [pieces], [pieces]
    for step in range(heads_axis // 4):
        ahead.append(lax.ppermute(ahead[-1], "head", right))
        behind.append(lax.ppermute(behind[-1], "head", left))

    q0 = queries[0].reshape(rows * heads, width)
    keys0 = latent_cache.reshape(rows * positions, width)
    row_of = lax.broadcasted_iota(jnp.int32, (rows, 1, rows, positions), 0)
    key_of = lax.broadcasted_iota(jnp.int32, (rows, 1, rows, positions), 2)
    spot = lax.broadcasted_iota(jnp.int32, (rows, 1, rows, positions), 3)
    mask0 = (row_of == key_of) & (spot < lengths[:, None, None, None])
    mask0 = jnp.broadcast_to(mask0, (rows, heads, rows, positions)).reshape(
        rows * heads, rows * positions
    )
    scores0 = jnp.where(mask0, dot(q0, keys0, ((1,), (1,))) * SCORE_SCALE, LOW)
    attn0 = softmax_values([(scores0, mask0, keys0[:, :KVR])]).astype(BF)

    def answers_of(parts):
        summed = lax.psum_scatter(parts, "head", scatter_dimension=1, tiled=True)
        return summed.reshape(groups, CAP, feats)

    def combine(s, back):
        back = back.reshape(groups * CAP, feats).astype(F32)
        mixed = dot(mix_of(expert_ids[s], route_score[s], groups), back, ((1,), (0,)), precision=lax.Precision.HIGHEST)
        return (tokens[s].astype(F32) + mixed).astype(BF)

    answers0 = answers_of(parts0)
    answers1 = answers_of(parts1)
    layer0 = combine(0, exchange(answers0, "expert"))

    part = jnp.dot(layer0, w_latent, preferred_element_type=F32).astype(BF)
    part, ahead[-1], behind[-1] = together(part, ahead[-1], behind[-1])
    for step in range(heads_axis // 4):
        ahead.append(lax.ppermute(ahead[-1], "head", right))
        if step + 1 < heads_axis // 4:
            behind.append(lax.ppermute(behind[-1], "head", left))
    whole_sum = everywhere(part).astype(F32).sum(axis=0)
    leading = whole_sum[:, :KVR]
    norm = lax.rsqrt(jnp.mean(leading * leading, axis=1, keepdims=True) + NORM_EPS)
    latent = jnp.concatenate(
        [
            (leading * norm * kv_gain).astype(BF),
            whole_sum[:, KVR:width].astype(BF),
            alive.astype(BF)[:, None] * eye,
        ],
        axis=1,
    )
    sent = dot(target, jnp.pad(latent, ((0, 0), (0, 1024 - wide))), ((0,), (0,))).astype(BF)
    answers1, ahead[-2], behind[-1] = together(answers1, ahead[-2], behind[-1])
    caches = ahead + behind[1:]
    last = exchange(
        jnp.concatenate([answers1, sent.reshape(groups, CAP, 1024 // CAP)], axis=2), "expert"
    )
    layer1 = combine(1, last[:, :, :feats])
    fresh = last[:, :, feats:].reshape(groups, 1024)[:, :wide]

    q1 = jnp.pad(queries[1].reshape(rows * heads, width), ((0, 0), (0, wide - width)))
    attn = pl.pallas_call(
        attend_kernel,
        out_shape=jax.ShapeDtypeStruct((STEPS, rows * heads, KVR), BF),
        in_specs=[pl.BlockSpec(memory_space=pltpu.VMEM)] * (3 + len(caches)),
        out_specs=pl.BlockSpec(memory_space=pltpu.VMEM),
        compiler_params=pltpu.CompilerParams(vmem_limit_bytes=32 * 2**20),
    )(attn0, q1, fresh, *caches)
    return attn.reshape(STEPS, rows, heads, KVR), jnp.stack([layer0, layer1])


def solution(mesh):
    return jax.shard_map(
        on_device,
        mesh=mesh,
        in_specs=(
            P(None, "expert", "head"),
            P(None, "expert", "head", None),
            P("expert", None, None),
            P("expert"),
            P(None, "expert", None),
            P(None, "expert", None),
            P(None, "expert"),
            P(None, "expert"),
            P("expert", None, "head"),
            P("expert", None, "head"),
            P("expert", "head", None),
            P("head", None),
            P(),
        ),
        out_specs=(P(None, "expert", "head", None), P(None, "expert", "head")),
        check_vma=False,
    )
```

```python
import jax
import jax.numpy as jnp
from jax import lax
from jax.experimental import pallas as pl
from jax.experimental.pallas import tpu as pltpu
from jax.sharding import PartitionSpec as P

KVR = 512
TOPK = 8
STEPS = 2
CAP = 4
ROWS = 24
LAT = 576
CACHE = 16
LANES = 128

SCORE_SCALE = 192.0 ** (-0.5)
ROUTE_SCALE = 2.5
NORM_EPS = 1e-06
LOW = -1e30

BF = jnp.bfloat16
F32 = jnp.float32


def dot(a, b, dims, precision=None):
    return lax.dot_general(a, b, (dims, ((), ())), precision=precision, preferred_element_type=F32)


def exchange(x, axis):
    return lax.all_to_all(x, axis, split_axis=0, concat_axis=0, tiled=True)


def together(*arrays):
    return lax.optimization_barrier(arrays)


def places_of(ids, groups, per):
    rows = ids.shape[0]
    column = lax.broadcasted_iota(jnp.int32, (1, 1, groups * per), 2)
    hit = ids[:, :, None] == column // per
    named = jnp.any(hit, axis=1)
    earlier = (
        lax.broadcasted_iota(jnp.int32, (rows, rows), 1)
        < lax.broadcasted_iota(jnp.int32, (rows, rows), 0)
    ).astype(BF)
    before = dot(earlier, named.astype(BF), ((1,), (0,)))
    return named & (before == (column[0] % CAP).astype(F32)), hit


def mix_of(ids, score, groups):
    place, hit = places_of(ids, groups, CAP)
    share = ROUTE_SCALE * score / jnp.sum(score, axis=1, keepdims=True)
    weight = jnp.sum(jnp.where(hit, share[:, :, None], 0.0), axis=1)
    return jnp.where(place, weight, 0.0)


def softmax_values(parts):
    top = parts[0][0].max(axis=1, keepdims=True)
    for scores, _, _ in parts[1:]:
        top = jnp.maximum(top, scores.max(axis=1, keepdims=True))
    terms = [jnp.where(mask, jnp.exp(scores - top), 0.0) for scores, mask, _ in parts]
    total = sum(t.sum(axis=1, keepdims=True) for t in terms)
    total = jnp.where(total > 0, total, 1.0)
    return sum(
        dot((t / total).astype(BF), values, ((1,), (0,)))
        for t, (_, _, values) in zip(terms, parts)
    )


def expert_kernel(x, gate_w, up_w, down_w, out, x_in, wide_w, narrow_w, made, *sems):
    feats, block = gate_w.shape[1:]
    count = out.shape[0]
    rows, span = x_in.shape
    step = feats // 4
    starts = range(0, feats, step)

    def fetch(k, source, target):
        copy = pltpu.make_async_copy(source, target, sems[k])
        copy.start()
        return copy

    lots, gates, ups = [], [], []
    for c, at in enumerate(starts):
        part = pl.ds(at, step)
        if at < span:
            lots.append(fetch(c, x.at[:, part], x_in.at[:, part]))
        gates.append(fetch(4 + c, gate_w.at[0, part], wide_w.at[part, pl.ds(0, block)]))
        ups.append(fetch(8 + c, up_w.at[0, part], wide_w.at[part, pl.ds(block, block)]))
    narrow = fetch(12, down_w.at[0], narrow_w)
    sums = [0.0] * (feats // span)
    for c, at in enumerate(starts):
        if at < span:
            lots[c].wait()
        gates[c].wait()
        ups[c].wait()
        lanes = at % span
        sums[at // span] += jnp.dot(
            x_in[:, lanes : lanes + step], wide_w[at : at + step], preferred_element_type=F32
        )
    total = sums[0]
    if len(sums) == 2:
        total = total + jnp.concatenate([sums[1][CAP:], sums[1][:CAP]], axis=0)
    hidden = (jax.nn.silu(total[:, :block]) * total[:, block:]).astype(BF)
    if len(sums) == 2:
        line = lax.broadcasted_iota(jnp.int32, (count, rows), 0)
        column = lax.broadcasted_iota(jnp.int32, (count, rows), 1)
        keep = (line + line // CAP * CAP == column).astype(BF)
        hidden = jnp.dot(keep, hidden, preferred_element_type=F32).astype(BF)
    narrow.wait()
    sent = []
    for c, at in enumerate(starts):
        made[:, at : at + step] = jnp.dot(
            hidden, narrow_w[:, at : at + step], preferred_element_type=F32
        ).astype(BF)
        part = pl.ds(at, step)
        sent.append(fetch(13 + c, made.at[:, part], out.at[:, part]))
    for copy in sent:
        copy.wait()


def expert_part(x, span, count, w_gate, w_up, w_down, *waits):
    feats, block = w_gate.shape[1:]

    def kernel(*refs):
        refs = refs[:4] + refs[4 + len(waits) :]
        expert_kernel(*refs)

    return pl.pallas_call(
        kernel,
        out_shape=jax.ShapeDtypeStruct((count, feats), BF),
        in_specs=[pl.BlockSpec(memory_space=pltpu.HBM)] * (4 + len(waits)),
        out_specs=pl.BlockSpec(memory_space=pltpu.HBM),
        scratch_shapes=[
            pltpu.VMEM((x.shape[0], span), BF),
            pltpu.VMEM((feats, 2 * block), BF),
            pltpu.VMEM((block, feats), BF),
            pltpu.VMEM((count, feats), BF),
        ]
        + [pltpu.SemaphoreType.DMA] * 17,
        compiler_params=pltpu.CompilerParams(vmem_limit_bytes=60 * 2**20),
        cost_estimate=pl.CostEstimate(
            flops=6 * count * feats * block,
            bytes_accessed=4 * count * feats + 6 * feats * block,
            transcendentals=count * block,
        ),
    )(x, w_gate, w_up, w_down, *waits)


def pack_kernel(places, tokens, targets, tiles, out):
    feats = tokens.shape[2]
    half = tokens.shape[0] // 2
    for c in range(half):
        lines = sum(
            jnp.dot(places[h], tokens[h * half + c], preferred_element_type=F32) for h in range(2)
        )
        out[:, c * feats : (c + 1) * feats] = lines.astype(BF)
    out[:, half * feats :] = jnp.dot(
        targets[...], tiles[...], preferred_element_type=F32
    ).astype(BF)


def collect_kernel(blocks, out, x, sem):
    lines, lanes = x.shape
    copy = pltpu.make_async_copy(blocks.at[:, pl.ds(blocks.shape[1] - lanes, lanes)], x, sem)
    copy.start()
    copy.wait()
    own = (
        lax.broadcasted_iota(jnp.int32, (ROWS, LANES), 1)
        == lax.broadcasted_iota(jnp.int32, (ROWS, LANES), 0) + (LAT - KVR)
    ).astype(BF)
    marked = (dot(own, x[:, LANES:], ((1,), (1,))) > 0.5).astype(BF)
    block = (
        lax.broadcasted_iota(jnp.int32, (lines, lines), 0) // 8
        == lax.broadcasted_iota(jnp.int32, (lines, lines), 1) // 8
    ).astype(BF)
    chosen = dot(marked, block, ((1,), (0,)))
    place = lax.broadcasted_iota(jnp.int32, (ROWS, lines), 1) % 8
    picks = [jnp.where((place == q) & (chosen > 0.5), 1.0, 0.0).astype(BF) for q in range(8)]
    found = [dot(pick, x[:, :LANES], ((1,), (0,))) for pick in picks]
    found += [dot(pick, x[:, LANES:], ((1,), (0,))) for pick in picks[: CACHE // 8]]
    out[...] = jnp.concatenate(found, axis=0).astype(BF)


def attend_kernel(earlier, query, fresh, *refs):
    caches, out = refs[:-1], refs[-1]
    out[0] = earlier[...]
    rows, wide = query.shape
    lanes = wide - KVR
    slot = lax.broadcasted_iota(jnp.int32, (rows, lanes), 0) // (rows // ROWS)
    lane = lax.broadcasted_iota(jnp.int32, (rows, lanes), 1)
    own = (lane == slot + (LAT - KVR)).astype(BF)
    tiles = KVR // lanes
    held = [x[...] for x in caches] if len(caches) > 1 else [caches[0][h] for h in range(8)]
    share = held[0].shape[0] // ROWS // (tiles + 1)
    values, rests = [], []
    for x in held:
        x = [x[at : at + ROWS] for at in range(0, x.shape[0], ROWS)]
        for p in range(share):
            values.append(jnp.concatenate(x[p * tiles : (p + 1) * tiles], axis=1))
            rests.append(x[share * tiles + p])
    old = jnp.concatenate(
        [jnp.concatenate(values, axis=0), jnp.concatenate(rests, axis=0)], axis=1
    )
    parts = []
    for keys in (old, fresh[...]):
        scores = dot(query[...], keys, ((1,), (1,))) * SCORE_SCALE
        mask = dot(own, keys[:, KVR:], ((1,), (1,))) > 0.5
        parts.append((jnp.where(mask, scores, LOW), mask, keys[:, :KVR]))
    out[1] = softmax_values(parts).astype(BF)


def on_device(
    tokens,
    queries,
    latent_cache,
    lengths,
    expert_ids,
    route_score,
    survive,
    destination,
    w_gate,
    w_up,
    w_down,
    w_latent,
    kv_gain,
):
    groups = lax.axis_size("expert")
    heads_axis = lax.axis_size("head")
    rows, positions, width = latent_cache.shape
    heads = queries.shape[2]
    feats = tokens.shape[2]
    wide = 640

    place, _ = places_of(expert_ids[0], groups, CAP)
    sending = dot(place.astype(BF), tokens[0], ((0,), (0,))).astype(BF)
    arrived0 = exchange(sending.reshape(groups, CAP, feats), "expert")
    rows0 = lax.all_gather(arrived0.reshape(groups * CAP, feats), "head", axis=1, tiled=True)

    def everywhere(x):
        return exchange(jnp.broadcast_to(x[None], (heads_axis,) + x.shape), "head")

    alive = survive[0] == 1
    eye = jnp.eye(rows, LANES - (width - KVR), dtype=BF)
    target = (destination[0][:, None] == jnp.arange(groups)[None, :]).astype(BF)
    share = positions // heads_axis
    tiles = KVR // LANES
    per = share * tiles
    first = lax.axis_index("head") * share
    held = lax.dynamic_slice_in_dim(latent_cache, first, share, axis=1)
    spot = first + lax.broadcasted_iota(jnp.int32, (rows, share), 1)
    valid = ((spot < lengths[:, None]) & alive[:, None]).astype(BF)
    rest = jnp.concatenate([held[:, :, KVR:], valid[:, :, None] * eye[:, None, :]], axis=2)
    rest = jnp.pad(rest, ((0, 0), (0, per - share), (0, 0)))
    cache_tiles = jnp.concatenate([held[:, :, :KVR].reshape(rows, per, LANES), rest], axis=2)
    cache_tiles = cache_tiles.transpose(1, 0, 2).reshape(per * rows, 2 * LANES)

    column = lax.broadcasted_iota(jnp.int32, (1, groups * per), 1)
    place8, _ = places_of(expert_ids[1], groups, per)
    places = jnp.stack(
        [jnp.where(column % per // CAP == h, place8, False).astype(BF).T for h in range(2)]
    )
    to = destination[0][:, None] == column // per
    targets = jnp.stack([to & (column % per == q) for q in range(per)])
    targets = targets.reshape(per * rows, groups * per).astype(BF).T

    own, arrived0, places, targets, cache_tiles = together(
        tokens[1], arrived0, places, targets, cache_tiles
    )
    both = pl.pallas_call(
        pack_kernel,
        out_shape=jax.ShapeDtypeStruct(
            (groups * per, heads_axis * feats // 2 + 2 * LANES), BF
        ),
        in_specs=[pl.BlockSpec(memory_space=pltpu.VMEM)] * 4,
        out_specs=pl.BlockSpec(memory_space=pltpu.VMEM),
        compiler_params=pltpu.CompilerParams(vmem_limit_bytes=32 * 2**20),
    )(places, everywhere(own), targets, cache_tiles)
    both = exchange(both.reshape(groups, per, both.shape[1]), "expert")
    both = both.reshape(groups * per, both.shape[2])

    parts0 = expert_part(rows0, heads_axis * feats, groups * CAP, w_gate, w_up, w_down)
    parts1 = expert_part(
        both, heads_axis * feats // 2, groups * CAP, w_gate, w_up, w_down, parts0
    )

    both, parts1 = together(both, parts1)
    pieces = pl.pallas_call(
        collect_kernel,
        out_shape=jax.ShapeDtypeStruct(((per + share) * rows, LANES), BF),
        in_specs=[pl.BlockSpec(memory_space=pltpu.HBM)],
        out_specs=pl.BlockSpec(memory_space=pltpu.VMEM),
        scratch_shapes=[pltpu.VMEM((groups * per, 2 * LANES), BF), pltpu.SemaphoreType.DMA],
    )(both)
    right = [(i, (i + 1) % heads_axis) for i in range(heads_axis)]
    left = [(i, (i - 1) % heads_axis) for i in range(heads_axis)]
    ahead, behind = [pieces], [pieces]
    for step in range(heads_axis // 4):
        ahead.append(lax.ppermute(ahead[-1], "head", right))
        behind.append(lax.ppermute(behind[-1], "head", left))

    q0 = queries[0].reshape(rows * heads, width)
    keys0 = latent_cache.reshape(rows * positions, width)
    row_of = lax.broadcasted_iota(jnp.int32, (rows, 1, rows, positions), 0)
    key_of = lax.broadcasted_iota(jnp.int32, (rows, 1, rows, positions), 2)
    spot = lax.broadcasted_iota(jnp.int32, (rows, 1, rows, positions), 3)
    mask0 = (row_of == key_of) & (spot < lengths[:, None, None, None])
    mask0 = jnp.broadcast_to(mask0, (rows, heads, rows, positions)).reshape(
        rows * heads, rows * positions
    )
    scores0 = jnp.where(mask0, dot(q0, keys0, ((1,), (1,))) * SCORE_SCALE, LOW)
    attn0 = softmax_values([(scores0, mask0, keys0[:, :KVR])]).astype(BF)

    def answers_of(parts):
        summed = lax.psum_scatter(parts, "head", scatter_dimension=1, tiled=True)
        return summed.reshape(groups, CAP, feats)

    def combine(s, back):
        back = back.reshape(groups * CAP, feats).astype(F32)
        mixed = dot(mix_of(expert_ids[s], route_score[s], groups), back, ((1,), (0,)), precision=lax.Precision.HIGHEST)
        return (tokens[s].astype(F32) + mixed).astype(BF)

    answers0 = answers_of(parts0)
    answers1 = answers_of(parts1)
    layer0 = combine(0, exchange(answers0, "expert"))

    part = jnp.dot(layer0, w_latent, preferred_element_type=F32).astype(BF)
    part, ahead[-1], behind[-1] = together(part, ahead[-1], behind[-1])
    for step in range(heads_axis // 4):
        ahead.append(lax.ppermute(ahead[-1], "head", right))
        if step + 1 < heads_axis // 4:
            behind.append(lax.ppermute(behind[-1], "head", left))
    whole_sum = everywhere(part).astype(F32).sum(axis=0)
    leading = whole_sum[:, :KVR]
    norm = lax.rsqrt(jnp.mean(leading * leading, axis=1, keepdims=True) + NORM_EPS)
    latent = jnp.concatenate(
        [
            (leading * norm * kv_gain).astype(BF),
            whole_sum[:, KVR:width].astype(BF),
            alive.astype(BF)[:, None] * eye,
        ],
        axis=1,
    )
    sent = dot(target, jnp.pad(latent, ((0, 0), (0, 1024 - wide))), ((0,), (0,))).astype(BF)
    answers1, ahead[-2], behind[-1] = together(answers1, ahead[-2], behind[-1])
    caches = ahead + behind[1:]
    last = exchange(
        jnp.concatenate([answers1, sent.reshape(groups, CAP, 1024 // CAP)], axis=2), "expert"
    )
    layer1 = combine(1, last[:, :, :feats])
    fresh = last[:, :, feats:].reshape(groups, 1024)[:, :wide]

    q1 = jnp.pad(queries[1].reshape(rows * heads, width), ((0, 0), (0, wide - width)))
    attn = pl.pallas_call(
        attend_kernel,
        out_shape=jax.ShapeDtypeStruct((STEPS, rows * heads, KVR), BF),
        in_specs=[pl.BlockSpec(memory_space=pltpu.VMEM)] * (3 + len(caches)),
        out_specs=pl.BlockSpec(memory_space=pltpu.VMEM),
        compiler_params=pltpu.CompilerParams(vmem_limit_bytes=32 * 2**20),
    )(attn0, q1, fresh, *caches)
    return attn.reshape(STEPS, rows, heads, KVR), jnp.stack([layer0, layer1])


def solution(mesh):
    return jax.shard_map(
        on_device,
        mesh=mesh,
        in_specs=(
            P(None, "expert", "head"),
            P(None, "expert", "head", None),
            P("expert", None, None),
            P("expert"),
            P(None, "expert", None),
            P(None, "expert", None),
            P(None, "expert"),
            P(None, "expert"),
            P("expert", None, "head"),
            P("expert", None, "head"),
            P("expert", "head", None),
            P("head", None),
            P(),
        ),
        out_specs=(P(None, "expert", "head", None), P(None, "expert", "head")),
        check_vma=False,
    )
```
